128 devices in a mesh: pts: 64 (over x, y, z), grp: 2 (over core).
Axes of the slice: x: 4, y: 4, z: 4, core: 2. Of those that a mesh axis runs over, the one named last changes fastest.
Arguments:
- mesh_samples: bfloat16 [1048576, 256], P(('pts', 'grp')), may hold values from -6 to 6
- upstream_derivative: bfloat16 [1048576, 256], P(('pts', 'grp')), may hold values from -6 to 6
- group_skin_region: int32 [64, 2, 16], replicated, may hold values from 0 to 511
- chip_group_tally: int32 [64, 2], replicated, may hold values from 1 to 16, as said below
- region_vector_lookup: bfloat16 [512, 256], replicated, may hold values from -3 to 3
- entry_matrix: bfloat16 [256, 512], replicated, may hold values from -0.375 to 0.375
- partition_matrix: bfloat16 [32, 64], replicated, may hold values from -1 to 1
- softmax_sharpness: float32 [8], replicated, may hold values from 0.25 to 2
- triple_mapping_matrix: bfloat16 [32, 96], replicated, may hold values from -1 to 1
- exit_matrix: bfloat16 [256, 256], replicated, may hold values from -0.375 to 0.375
Outputs:
- grad_points: bfloat16 [1048576, 256], P(('pts', 'grp'))
- grad_patch: float32 [512, 256], replicated
- grad_w_in: float32 [256, 512], replicated
- grad_w_slice: float32 [32, 64], replicated
- grad_temperature: float32 [8], replicated
- grad_w_qkv: float32 [32, 96], replicated
- grad_w_out: float32 [256, 256], replicated
The draws below stay inside these ranges and needn't reach their ends.
Inputs may be any that keep to these rules, and one draw needn't show every extreme that they name: `chip_group_tally`: the points of a device fill its first row blocks; in every draw some device holds 16 blocks.
All inputs are finite; a program needn't handle non-finite values.
Results may differ from the reference program's by a relative error of at most 0.012.
The reference program's roundings to bfloat16 on the way count: a program that leaves them out, or rounds other values in their place, can miss the bound.
Values may be sent and summed in bfloat16 or wider, within the bound.
No kernel may reach another device: no remote copies, remote signals or barrier semaphores. Data moves between devices by JAX's collectives and lax.ppermute only.
A program may use at most 192 MiB of HBM per device.

```python
import math
import jax
import jax.numpy as jnp
from jax import lax

C = 256
FOCUS_CHANNELS = 8
SLICES = 64
HEAD_DIM = 32
PATCHES = 512
BLOCK_ROWS = 512
BLOCKS = 16
TOKENS = 1048576
N_PTS = 64
N_GRP = 2


def draw_chip_group_tally(key, part):
    key = jax.random.fold_in(key, 7)
    key_small, key_start = jax.random.split(key, 2)
    run = max(1, N_PTS // 4)
    small = jax.random.randint(key_small, (N_PTS, N_GRP), 1, BLOCKS // 2 + 1)
    start = jax.random.randint(key_start, (), 0, N_PTS)
    position = jnp.arange(N_PTS, dtype=jnp.int32)
    heavy = jnp.mod(position - start, N_PTS) < run
    counts = jnp.where(heavy[:, None], BLOCKS, small)
    return counts.astype(jnp.int32)


def with_ends(array, own_key, smallest, high):
    dims = array.shape
    place = [jax.random.randint(jax.random.fold_in(own_key, axis), (), 0, dims[axis]) for axis in range(len(dims))]
    array = array.at[tuple(place)].set(smallest)
    longest = dims.index(max(dims))
    place[longest] = (place[longest] + 1) % dims[longest]
    return array.at[tuple(place)].set(high)


def shard_levels(own_key, shape, cuts, smallest, top_value):
    def one(dim, blocks):
        draws = jax.random.uniform(jax.random.fold_in(jax.random.fold_in(own_key, 6), dim), (blocks,), jnp.float32, smallest / len(cuts), top_value / len(cuts))
        return jnp.repeat(jnp.exp(draws), shape[dim] // blocks).reshape((-1,) + (1,) * (len(shape) - dim - 1))

    loudness = one(*cuts[0])
    for cut in cuts[1:]:
        loudness = loudness * one(*cut)
    return loudness


def noise(key, dims, width, limit, shards=(), held_as=jnp.bfloat16):
    factor_of = shard_levels(key, dims, shards, -0.22, 0.18) if shards else 1.0
    result = jax.random.normal(key, dims, jnp.float32) * width * factor_of
    return jnp.minimum(jnp.maximum(result, -limit), limit).astype(held_as)


def setup_inputs(seed: int = 0) -> dict:
    streams_of = jax.random.split(jax.random.key(seed), 11)
    mesh_samples = noise(streams_of[0], (TOKENS, C), 1.0, 6.0, ((0, 128),))
    upstream_derivative = noise(streams_of[1], (TOKENS, C), 1.0, 6.0, ((0, 128),))
    group_skin_region = with_ends(jax.random.randint(streams_of[2], (N_PTS, N_GRP, BLOCKS), 0, PATCHES), jax.random.fold_in(streams_of[2], 1), 0, PATCHES - 1).astype(jnp.int32)
    chip_group_tally = draw_chip_group_tally(jax.random.fold_in(streams_of[10], 71), 0)
    region_vector_lookup = noise(streams_of[4], (PATCHES, C), 0.5, 3.0)
    entry_matrix = noise(streams_of[5], (C, 2 * C), C ** -0.5, 0.375)
    partition_matrix = noise(streams_of[6], (HEAD_DIM, SLICES), HEAD_DIM ** -0.5, 1.0)
    softmax_sharpness = jnp.clip(jnp.exp(jax.random.uniform(streams_of[7], (FOCUS_CHANNELS,), jnp.float32, math.log(0.25), math.log(2.0))), 0.25, 2.0)
    triple_mapping_matrix = noise(streams_of[8], (HEAD_DIM, 3 * HEAD_DIM), HEAD_DIM ** -0.5, 1.0)
    exit_matrix = noise(streams_of[9], (C, C), C ** -0.5, 0.375)
    return dict(mesh_samples=mesh_samples, upstream_derivative=upstream_derivative, group_skin_region=group_skin_region, chip_group_tally=chip_group_tally, region_vector_lookup=region_vector_lookup, entry_matrix=entry_matrix, partition_matrix=partition_matrix, softmax_sharpness=softmax_sharpness, triple_mapping_matrix=triple_mapping_matrix, exit_matrix=exit_matrix)


EPS = 1e-05
HIGH = lax.Precision.HIGHEST

def attend(token, w_qkv_f):
    head_dim = token.shape[-1]
    qkv = jnp.einsum('hgd,de->hge', token, w_qkv_f, precision=HIGH)
    query = qkv[..., :head_dim]
    keys = qkv[..., head_dim:2 * head_dim]
    values = qkv[..., 2 * head_dim:]
    scores = jnp.einsum('hgd,hkd->hgk', query, keys, precision=HIGH) / math.sqrt(head_dim)
    probs = jax.nn.softmax(scores, axis=-1)
    return jnp.einsum('hgk,hkd->hgd', probs, values, precision=HIGH)

def slice_middle(norm, raw, grad_otb, triple_mapping_matrix):
    denom = norm + EPS
    token = raw / denom[..., None]
    out_tok, pullback = jax.vjp(attend, token, triple_mapping_matrix.astype(jnp.float32))
    grad_token, derivative_triple_matrix = pullback(grad_otb)
    unnormalized_gradient = (grad_token / denom[..., None]).astype(jnp.bfloat16)
    gradient_of_norm = -lax.optimization_barrier(jnp.sum(grad_token * token, axis=-1)) / denom
    return (out_tok.astype(jnp.bfloat16), unnormalized_gradient, gradient_of_norm, derivative_triple_matrix)

def reference(mesh_samples, upstream_derivative, group_skin_region, chip_group_tally, region_vector_lookup, entry_matrix, partition_matrix, softmax_sharpness, triple_mapping_matrix, exit_matrix):
    devices = N_PTS * N_GRP
    rows_dev = BLOCKS * BLOCK_ROWS
    head_dim = C // FOCUS_CHANNELS
    x_dev = mesh_samples.reshape(devices, rows_dev, C)
    cot_dev = upstream_derivative.reshape(devices, rows_dev, C)
    patch_dev = group_skin_region.reshape(devices, BLOCKS)
    count_dev = chip_group_tally.reshape(devices)
    block_of_row = (jnp.arange(rows_dev) // BLOCK_ROWS).astype(jnp.int32)
    partition_matrix_wide = partition_matrix.astype(jnp.float32)

    def prepare(x_rows, patch_ids, count):
        valid = (block_of_row < count).astype(jnp.float32)
        row_patch = jnp.take(patch_ids, block_of_row)
        patch_rows = jnp.take(region_vector_lookup, row_patch, axis=0)
        input_points = (x_rows.astype(jnp.float32) + patch_rows.astype(jnp.float32)).astype(jnp.bfloat16)
        mapped_source = jnp.dot(input_points, entry_matrix, preferred_element_type=jnp.float32).astype(jnp.bfloat16)
        hidden_activations = mapped_source[:, :C].reshape(rows_dev, FOCUS_CHANNELS, head_dim).astype(jnp.float32)
        fx = mapped_source[:, C:].reshape(rows_dev, FOCUS_CHANNELS, head_dim).astype(jnp.float32)
        membership_raw_scores = jnp.einsum('xzm,mg->xzg', hidden_activations, partition_matrix_wide) / softmax_sharpness[None, :, None]
        weights = jax.nn.softmax(membership_raw_scores, axis=-1) * valid[:, None, None]
        return (input_points, row_patch, hidden_activations, fx, membership_raw_scores, weights)

    def grad_y_of(cotangent_row_values):
        grad_y = lax.dot_general(cotangent_row_values, exit_matrix, (((1,), (1,)), ((), ())), preferred_element_type=jnp.float32)
        return grad_y.astype(jnp.bfloat16).reshape(rows_dev, FOCUS_CHANNELS, head_dim).astype(jnp.float32)

    def first(running_state, item):
        x_rows, cotangent_row_values, patch_ids, count = item
        input_points, row_patch, hidden_activations, fx, membership_raw_scores, weights = prepare(x_rows, patch_ids, count)
        weights_bf = weights.astype(jnp.bfloat16).astype(jnp.float32)
        grad_y = grad_y_of(cotangent_row_values)
        norm = running_state[0] + lax.optimization_barrier(jnp.sum(weights, axis=0))
        raw = running_state[1] + jnp.einsum('rhg,rhd->hgd', weights_bf, fx)
        gsum = running_state[2] + jnp.einsum('rhg,rhd->hgd', weights_bf, grad_y)
        return ((norm, raw, gsum), None)
    zero_sums = (jnp.zeros((FOCUS_CHANNELS, SLICES), jnp.float32), jnp.zeros((FOCUS_CHANNELS, SLICES, head_dim), jnp.float32), jnp.zeros((FOCUS_CHANNELS, SLICES, head_dim), jnp.float32))
    (norm, raw, grad_otb), _ = lax.scan(first, zero_sums, (x_dev, cot_dev, patch_dev, count_dev))
    output_bias_rows, unnormalized_gradient, gradient_of_norm, derivative_triple_matrix = slice_middle(norm, raw, grad_otb, triple_mapping_matrix)
    out_f = output_bias_rows.astype(jnp.float32)
    grad_raw_f = unnormalized_gradient.astype(jnp.float32)

    def second(running_state, item):
        x_rows, cotangent_row_values, patch_ids, count = item
        input_points, row_patch, hidden_activations, fx, membership_raw_scores, weights = prepare(x_rows, patch_ids, count)
        weights_bf = weights.astype(jnp.bfloat16).astype(jnp.float32)
        mixed = jnp.einsum('rhg,hgd->rhd', weights_bf, out_f).astype(jnp.bfloat16).reshape(rows_dev, C)
        derivative_leaving = lax.dot_general(mixed, cotangent_row_values, (((0,), (0,)), ((), ())), preferred_element_type=jnp.float32)
        grad_y = grad_y_of(cotangent_row_values)
        grad_w = jnp.einsum('rhd,hgd->rhg', grad_y, out_f) + jnp.einsum('rhd,hgd->rhg', fx, grad_raw_f) + gradient_of_norm[None]
        derivative_raw_membership = weights * (grad_w - lax.optimization_barrier(jnp.sum(weights * grad_w, axis=-1, keepdims=True)))
        sharpness_derivative = -lax.optimization_barrier(jnp.sum(derivative_raw_membership * membership_raw_scores, axis=(0, 2))) / softmax_sharpness
        partition_derivative = (derivative_raw_membership / softmax_sharpness[None, :, None]).astype(jnp.bfloat16).astype(jnp.float32)
        derivative_partition = jnp.einsum('rhd,rhg->dg', hidden_activations, partition_derivative)
        grad_mid = jnp.einsum('rhg,dg->rhd', partition_derivative, partition_matrix_wide)
        grad_fx = jnp.einsum('rhg,hgd->rhd', weights_bf, grad_raw_f)
        grad_proj = jnp.concatenate([grad_mid.reshape(rows_dev, C), grad_fx.reshape(rows_dev, C)], axis=1).astype(jnp.bfloat16)
        derivative_entering = lax.dot_general(input_points, grad_proj, (((0,), (0,)), ((), ())), preferred_element_type=jnp.float32)
        derivative_layer_source = lax.dot_general(grad_proj, entry_matrix, (((1,), (1,)), ((), ())), preferred_element_type=jnp.float32)
        onehot = (row_patch[:, None] == jnp.arange(PATCHES)[None, :].astype(jnp.int32)).astype(jnp.float32)
        derivative_region = lax.dot_general(onehot, derivative_layer_source, (((0,), (0,)), ((), ())), precision=HIGH)
        updated_state = (running_state[0] + derivative_entering, running_state[1] + derivative_leaving, running_state[2] + derivative_partition, running_state[3] + sharpness_derivative, running_state[4] + derivative_region)
        return (updated_state, derivative_layer_source.astype(jnp.bfloat16))
    zero_grads = (jnp.zeros((C, 2 * C), jnp.float32), jnp.zeros((C, C), jnp.float32), jnp.zeros((head_dim, SLICES), jnp.float32), jnp.zeros((FOCUS_CHANNELS,), jnp.float32), jnp.zeros((PATCHES, C), jnp.float32))
    parameter_derivatives, grad_rows = lax.scan(second, zero_grads, (x_dev, cot_dev, patch_dev, count_dev))
    return (grad_rows.reshape(devices * rows_dev, C), parameter_derivatives[4], parameter_derivatives[0], parameter_derivatives[2], parameter_derivatives[3], derivative_triple_matrix, parameter_derivatives[1])
```

```python
import functools
import math

import jax
import jax.numpy as jnp
from jax import lax
from jax.experimental import pallas as pl
from jax.experimental.pallas import tpu as pltpu
from jax.sharding import PartitionSpec as P

f32 = jnp.float32
bf16 = jnp.bfloat16
HIGH = lax.Precision.HIGHEST
EPS = 1e-05
LOG2E = math.log2(math.e)

ROWS = 512
BLOCKS = 16
STEP = 1024
STEPS = BLOCKS * ROWS // STEP
C = 256
H = 8
D = 32
G = 64
HG = H * G
PATCHES = 512
SUMS = 136
MID = 224
PIECE = 176
HALF = 4 * PIECE
BUF = 2 * HALF
VMEM_LIMIT = 24 * 2**20
SMALL = pltpu.CompilerParams(vmem_limit_bytes=8 * 2**20)

NN = (((1,), (0,)), ((), ()))
NT = (((1,), (1,)), ((), ()))
TN = (((0,), (0,)), ((), ()))


def dot(a, b, dims, precision=None):
    return lax.dot_general(a, b, dims, precision=precision, preferred_element_type=f32)


def split(a):
    hi = a.astype(bf16)
    return hi, (a - hi.astype(f32)).astype(bf16)


def dot_left2(a, b, dims):
    hi, lo = split(a)
    return dot(hi, b, dims) + dot(lo, b, dims)


def dot_right2(a, b, dims):
    hi, lo = split(b)
    return dot(a, hi, dims) + dot(a, lo, dims)


def iota(shape, dim):
    return lax.broadcasted_iota(jnp.int32, shape, dim)


def head_mask(j, rows):
    return (iota((rows, 128), 1) >> 5) == j


def spread(packed):
    return jnp.concatenate([jnp.where(head_mask(j, G), packed, 0.0) for j in range(4)], axis=0)


def gather_heads(wide):
    total = jnp.where(head_mask(0, G), wide[0:G], 0.0)
    for j in range(1, 4):
        total = total + jnp.where(head_mask(j, G), wide[j * G : (j + 1) * G], 0.0)
    return total


def in_vmem():
    return pl.BlockSpec(memory_space=pltpu.VMEM)


def in_smem():
    return pl.BlockSpec(memory_space=pltpu.SMEM)


def in_hbm():
    return pl.BlockSpec(memory_space=pl.ANY)


def hbm(v):
    return pltpu.with_memory_space_constraint(v, pltpu.HBM)


def vmem(v):
    return pltpu.with_memory_space_constraint(v, pltpu.VMEM)


def place():
    return lax.axis_index("pts"), lax.axis_index("grp")


def block_count(tally_ref):
    pts, grp = place()
    return tally_ref[pts, grp]


def patch_onehot(region_ref):
    pts, grp = place()
    ids = region_ref[pts, pl.ds(grp, 1), :]
    return (iota((PATCHES, BLOCKS), 0) == ids).astype(f32)


def add_block_sums(ref, at, wide, b):
    lane = iota((G, 128), 1)
    old = ref[at, :]
    for k in range(2):
        lo = k * ROWS
        part = (wide[:, lo : lo + 128] + wide[:, lo + 128 : lo + 256]) + (
            wide[:, lo + 256 : lo + 384] + wide[:, lo + 384 : lo + 512]
        )
        old = jnp.where(lane == 2 * b + k, jnp.sum(part, axis=1, keepdims=True), old)
    ref[at, :] = old


def first_kernel(
    tally_ref,
    region_ref,
    temp_ref,
    x_hbm,
    u_hbm,
    lut_hbm,
    e_in_hbm,
    x_out_hbm,
    p_hbm,
    w_ref,
    fg_ref,
    xin_ref,
    u_ref,
    keep_ref,
    send_ref,
    cw_ref,
    pblk_ref,
    x_ref,
    lut_ref,
    e_in_ref,
    x_out_ref,
    p_ref,
    et_ref,
    rows_ref,
    acc_ref,
    x_sem,
    u_sem,
    sem,
):
    count = block_count(tally_ref)
    steps = (count + 1) >> 1
    small = [
        pltpu.make_async_copy(src, dst, sem.at[k])
        for k, (src, dst) in enumerate(
            (
                (e_in_hbm, e_in_ref),
                (p_hbm, p_ref),
                (lut_hbm, lut_ref),
                (x_out_hbm, x_out_ref),
            )
        )
    ]
    for copy in small:
        copy.start()

    def rows_copies(b):
        at = pl.ds(pl.multiple_of(b * STEP, STEP), STEP)
        return (
            pltpu.make_async_copy(x_hbm.at[at, :], x_ref.at[b], x_sem.at[b]),
            pltpu.make_async_copy(u_hbm.at[at, :], u_ref.at[b], u_sem.at[b]),
        )

    @pl.loop(0, steps)
    def _(b):
        for copy in rows_copies(b):
            copy.start()

    acc_ref[...] = jnp.zeros_like(acc_ref)
    cw_ref[...] = jnp.zeros_like(cw_ref)
    onehot = patch_onehot(region_ref).T.astype(bf16)
    for copy in small:
        copy.wait()
    et_ref[...] = e_in_ref[...].T
    t1 = ((iota((HG, G), 0) & (G - 1)) == iota((HG, G), 1)).astype(f32).astype(bf16)
    t2 = (iota((D, C), 0) == (iota((D, C), 1) & (D - 1))).astype(f32).astype(bf16)
    tall = dot(t1, p_ref[...], NT).astype(bf16)
    tiled = dot(tall, t2, NN)
    own = (iota((HG, C), 0) >> 6) == (iota((HG, C), 1) >> 5)
    pblk_ref[...] = jnp.where(own, tiled, 0.0).astype(bf16)
    rows_ref[...] = dot(onehot, lut_ref[...], NN)

    @pl.loop(0, steps)
    def _(b):
        for copy in rows_copies(b):
            copy.wait()
        for k in range(2):
            half = pl.ds(k * ROWS, ROWS)
            xin_ref[b, half, :] = (
                x_ref[b, half, :].astype(f32) + rows_ref[pl.ds(2 * b + k, 1), :]
            ).astype(bf16)
        proj = dot(et_ref[...], xin_ref[b], NT).astype(bf16)
        grad_y = dot(x_out_ref[...], u_ref[b], NT).astype(bf16)
        for q in range(2):
            fg_ref[b, 256 * q : 256 * q + 128, :] = proj[256 + 128 * q : 384 + 128 * q]
            fg_ref[b, 256 * q + 128 : 256 * q + 256, :] = grad_y[128 * q : 128 * q + 128]
        logits = dot(pblk_ref[...], proj[0:C], NN)
        valid = (iota((1, STEP), 1) + b * STEP < count * ROWS).astype(f32)
        for h in range(H):
            at = pl.ds(h * G, G)
            part = logits[G * h : G * h + G]
            scale = LOG2E / jnp.full((1, STEP), temp_ref[h], f32)
            top = jnp.max(part, axis=0, keepdims=True)
            ex = jnp.exp2((part - top) * scale)
            wt = ex * (valid / jnp.sum(ex, axis=0, keepdims=True))
            add_block_sums(cw_ref, at, wt, b)
            w_ref[b, at, :] = wt.astype(bf16)
        for q in range(2):
            at = pl.ds(256 * q, 256)
            acc_ref[q] += dot(w_ref[b, at, :], fg_ref[b, at, :], NT)

    core = lax.axis_index("grp")
    ones = jnp.ones((8, 128), f32)
    for q in range(2):
        raw = gather_heads(acc_ref[q, :, 0:128])
        grad = gather_heads(acc_ref[q, :, 128:256])
        norm = dot(ones, cw_ref[256 * q : 256 * q + 256, :], NT, HIGH)
        row = iota((8, 128), 0)
        norm = jnp.where(row == 0, norm[:, 0:128], jnp.where(row == 1, norm[:, 128:256], 0.0))

        def put(ref):
            ref[0:64, :] = raw
            ref[64:128, :] = grad
            ref[128:136, :] = norm

        pl.when(core == q)(lambda: put(keep_ref))
        pl.when(core != q)(lambda: put(send_ref))


def first_sweep(x, u, region, tally, lut, e_in, x_out, part, temp):
    return pl.pallas_call(
        first_kernel,
        in_specs=[in_smem(), in_vmem(), in_smem()] + [in_hbm()] * 6,
        out_specs=[in_vmem()] * 8,
        scratch_shapes=[
            pltpu.VMEM((STEPS, STEP, C), bf16),
            pltpu.VMEM((PATCHES, C), bf16),
            pltpu.VMEM((C, 2 * C), bf16),
            pltpu.VMEM((C, C), bf16),
            pltpu.VMEM((D, G), bf16),
            pltpu.VMEM((2 * C, C), bf16),
            pltpu.VMEM((BLOCKS, C), f32),
            pltpu.VMEM((2, 256, 256), f32),
            pltpu.SemaphoreType.DMA((STEPS,)),
            pltpu.SemaphoreType.DMA((STEPS,)),
            pltpu.SemaphoreType.DMA((4,)),
        ],
        out_shape=[
            pltpu.VMEM((STEPS, HG, STEP), bf16),
            pltpu.VMEM((STEPS, HG, STEP), bf16),
            pltpu.VMEM((STEPS, STEP, C), bf16),
            pltpu.VMEM((STEPS, STEP, C), bf16),
            jax.ShapeDtypeStruct((SUMS, 128), f32),
            jax.ShapeDtypeStruct((SUMS, 128), f32),
            jax.ShapeDtypeStruct((HG, 128), f32),
            jax.ShapeDtypeStruct((HG, C), bf16),
        ],
        compiler_params=pltpu.CompilerParams(vmem_limit_bytes=VMEM_LIMIT),
        name="first_sweep",
    )(tally, region, temp, *map(hbm, (x, u, lut, e_in, x_out, part)))


def moment_kernel(tally_ref, rows_ref, w_ref, y_ref):
    y_ref[...] = jnp.zeros_like(y_ref)

    @pl.loop(0, (block_count(tally_ref) + 1) >> 1)
    def _(b):
        y_ref[...] += dot(w_ref[b], rows_ref[b], NN)


def moment(name, tally, rows, w):
    return pl.pallas_call(
        moment_kernel,
        in_specs=[in_smem(), in_vmem(), in_vmem()],
        out_specs=in_vmem(),
        out_shape=jax.ShapeDtypeStruct((HG, C), f32),
        compiler_params=SMALL,
        cost_estimate=pl.CostEstimate(
            flops=2 * BLOCKS * ROWS * HG * C, bytes_accessed=8 * 2**20, transcendentals=0
        ),
        name=name,
    )(tally, vmem(rows), vmem(w))


def middle_kernel(s_ref, t_ref, out_ref):
    raw = s_ref[0:64, :]
    grad = s_ref[64:128, :]
    norm = jnp.concatenate([s_ref[128:136, :], jnp.zeros((120, 128), f32)], axis=0).T
    denom = jnp.full((G, 128), EPS, f32)
    for j in range(4):
        col = norm[G * (j % 2) : G * (j % 2) + G, j // 2 : j // 2 + 1]
        denom = denom + jnp.where(head_mask(j, G), col, 0.0)
    inv = 1.0 / denom
    token = raw * inv
    t2 = (iota((D, 128), 0) == (iota((D, 128), 1) & (D - 1))).astype(f32)
    own = (iota((128, 128), 0) >> 5) == (iota((128, 128), 1) >> 5)
    triple = t_ref[...].astype(f32)

    def diagonal(k):
        wide = dot(triple[:, D * k : D * k + D], t2, NN, HIGH)
        return jnp.where(own, jnp.concatenate([wide] * 4, axis=0), 0.0)

    wq, wk, wv = diagonal(0), diagonal(1), diagonal(2)
    query = dot(token, wq, NN, HIGH)
    keys = dot(token, wk, NN, HIGH)
    values = dot(token, wv, NN, HIGH)
    rate = 1.0 / math.sqrt(D)
    query_s = spread(query)
    scores = dot(query_s, keys, NT, HIGH) * rate
    scores = jnp.exp(scores - jnp.max(scores, axis=1, keepdims=True))
    probs = scores / jnp.sum(scores, axis=1, keepdims=True)
    out = gather_heads(dot(probs, values, NN, HIGH))
    grad_s = spread(grad)
    d_values = dot(probs.T, grad_s, NN, HIGH)
    d_probs = dot(grad_s, values, NT, HIGH)
    d_scores = probs * (d_probs - jnp.sum(d_probs * probs, axis=1, keepdims=True)) * rate
    d_query = gather_heads(dot(d_scores, keys, NN, HIGH))
    d_keys = dot(d_scores.T, query_s, NN, HIGH)
    d_token = (
        dot(d_query, wq, NT, HIGH) + dot(d_keys, wk, NT, HIGH) + dot(d_values, wv, NT, HIGH)
    )
    grad_raw = d_token * inv
    group = ((iota((128, 128), 0) >> 5) == iota((128, 128), 1)).astype(f32)
    first = (iota((128, 128), 1) < 4).astype(f32)
    grad_norm = -dot(d_token * token * inv, group * first, NN, HIGH)
    out_ref[0:64, :] = out.astype(bf16).astype(f32)
    out_ref[64:128, :] = grad_raw.astype(bf16).astype(f32)
    out_ref[128:192, :] = grad_norm
    token_t = jnp.concatenate([token, jnp.zeros((64, 128), f32)], axis=0).T[:, 0:64]
    total = jnp.zeros((D, 128), f32)
    for k, d_part in enumerate((d_query, d_keys, d_values)):
        full = jnp.where(own, dot(token_t, d_part, NN, HIGH), 0.0)
        full = full[0:32] + full[32:64] + (full[64:96] + full[96:128])
        fold = ((iota((128, 128), 0) & (D - 1)) + D * k == iota((128, 128), 1)).astype(f32)
        total = total + dot(full, fold, NN, HIGH)
    out_ref[192:224, :] = total


def middle(sums, triple):
    return pl.pallas_call(
        middle_kernel,
        out_shape=jax.ShapeDtypeStruct((MID, 128), f32),
        compiler_params=SMALL,
        name="middle",
    )(sums, triple)


def second_kernel(
    tally_ref,
    region_ref,
    temp_ref,
    temp_row_ref,
    xin_ref,
    w_ref,
    fg_ref,
    mine_ref,
    theirs_ref,
    e_in_ref,
    pblk_ref,
    p_ref,
    cw_ref,
    y_ref,
    z_ref,
    gs_ref,
    pq_ref,
    keep_ref,
    send_ref,
    og_ref,
    gn_ref,
    v_ref,
    cg_ref,
    ob_ref,
    gr_ref,
    buf_ref,
):
    steps = (block_count(tally_ref) + 1) >> 1
    core = lax.axis_index("grp")

    def prologue():
        for q in range(2):
            at = pl.ds(256 * q, 256)
            mine = core == q
            out_b = jnp.where(mine, mine_ref[0:64, :], theirs_ref[0:64, :])
            grad_raw = jnp.where(mine, mine_ref[64:128, :], theirs_ref[64:128, :])
            grad_norm = jnp.where(mine, mine_ref[128:192, :], theirs_ref[128:192, :])
            grad_norm = grad_norm - jnp.mean(grad_norm, axis=0, keepdims=True)
            for j in range(4):
                gn_ref[pl.ds(256 * q + G * j, G), :] = jnp.broadcast_to(
                    grad_norm[:, j : j + 1], (G, 128)
                )
            cols = pl.ds(128 * q, 128)
            off = slice(0, 256) if q else slice(256, 512)
            zero = jnp.zeros((256, 128), bf16)
            ob_ref[at, cols] = spread(out_b).astype(bf16)
            gr_ref[at, cols] = spread(grad_raw).astype(bf16)
            ob_ref[off, cols] = zero
            gr_ref[off, cols] = zero
            og_ref[at, 0:128] = spread(
                grad_raw - jnp.mean(grad_raw, axis=0, keepdims=True)
            ).astype(bf16)
            og_ref[at, 128:256] = spread(
                out_b - jnp.mean(out_b, axis=0, keepdims=True)
            ).astype(bf16)
        v_ref[...] = jnp.zeros_like(v_ref)
        cg_ref[...] = jnp.zeros_like(cg_ref)

    prologue()

    @pl.loop(0, steps)
    def _(b):
        for q in range(2):
            at = pl.ds(256 * q, 256)
            grad_w = dot(og_ref[at, :], fg_ref[b, at, :], NN)
            for j in range(4):
                h = 4 * q + j
                at = pl.ds(h * G, G)
                col = gn_ref[at, :]
                wt = w_ref[b, at, :].astype(f32)
                gw = grad_w[G * j : G * j + G] + jnp.concatenate([col] * (STEP // 128), axis=1)
                wg = wt * gw
                inv = 1.0 / jnp.full((1, STEP), temp_ref[h], f32)
                gs = (wg - wt * jnp.sum(wg, axis=0, keepdims=True)) * inv
                add_block_sums(cg_ref, at, gs, b)
                gs_ref[b, at, :] = gs.astype(bf16)
        v_ref[...] += dot(gs_ref[b], xin_ref[b], NN)

    v = v_ref[...]
    v_hi, v_lo = split(v)
    pblk = pblk_ref[...]
    gr = gr_ref[...]
    pq_ref[:, 0:512] = dot(e_in_ref[:, 0:256], pblk, NT).astype(bf16)
    pq_ref[:, 512:1024] = dot(e_in_ref[:, 256:512], gr, NT).astype(bf16)
    buf_ref[0:256, :] = dot_left2(v.T, pblk, NN)
    buf_ref[256:512, :] = dot_left2(y_ref[...].T, gr, NN)
    buf_ref[512:768, :] = dot_right2(ob_ref[...].astype(f32).T.astype(bf16), z_ref[...], NN)
    onehot = patch_onehot(region_ref).astype(bf16)
    per_block = dot_left2(cg_ref[...].T, pq_ref[:, 0:512], NT)
    per_block = per_block + dot_left2(cw_ref[...].T, pq_ref[:, 512:1024], NT)
    buf_ref[768:1280, :] = dot_right2(onehot, per_block[0:BLOCKS], NN)
    et = e_in_ref[:, 0:256].T
    cross = dot(et, v_hi, NT) + dot(et, v_lo, NT)
    own = (iota((256, 512), 0) >> 5) == (iota((256, 512), 1) >> 6)
    cross = jnp.where(own, cross, 0.0)
    heads = cross[0:32]
    for k in range(1, 8):
        heads = heads + cross[32 * k : 32 * k + 32]
    fold = ((iota((HG, 128), 0) & (G - 1)) == iota((HG, 128), 1)).astype(f32)
    tile = (iota((G, HG), 0) == (iota((G, HG), 1) & (G - 1))).astype(f32).astype(bf16)
    by_head = ((iota((HG, 8), 0) >> 6) == iota((HG, 8), 1)).astype(f32)
    weighed = heads * dot(p_ref[...], tile, NN)
    weighed = jnp.broadcast_to(jnp.sum(weighed, axis=0, keepdims=True), (8, HG))
    sharp = -dot(weighed, by_head, NN, HIGH) / temp_row_ref[...]
    buf_ref[1280:BUF, :] = jnp.zeros((BUF - 1280, 256), f32)
    buf_ref[1280:1312, 0:128] = dot(heads, fold, NN, HIGH)
    buf_ref[1312:1320, 0:8] = sharp
    keep_ref[...] = buf_ref[pl.ds(pl.multiple_of(core * HALF, 16), HALF), :]
    send_ref[...] = buf_ref[
        pl.ds(pl.multiple_of((1 - core) * HALF, 16), HALF), :
    ].astype(bf16)


def second_sweep(tally, region, temp, xin, w, fg, mine, theirs, e_in, pblk, part, cw, y, z):
    return pl.pallas_call(
        second_kernel,
        in_specs=[in_smem(), in_vmem(), in_smem()] + [in_vmem()] * 12,
        out_specs=[in_vmem()] * 4,
        scratch_shapes=[
            pltpu.VMEM((HG, 256), bf16),
            pltpu.VMEM((HG, 128), f32),
            pltpu.VMEM((HG, C), f32),
            pltpu.VMEM((HG, 128), f32),
            pltpu.VMEM((HG, C), bf16),
            pltpu.VMEM((HG, C), bf16),
            pltpu.VMEM((BUF, C), f32),
        ],
        out_shape=[
            pltpu.VMEM((STEPS, HG, STEP), bf16),
            jax.ShapeDtypeStruct((C, 1024), bf16),
            jax.ShapeDtypeStruct((HALF, C), f32),
            jax.ShapeDtypeStruct((HALF, C), bf16),
        ],
        compiler_params=pltpu.CompilerParams(vmem_limit_bytes=VMEM_LIMIT),
        name="second_sweep",
    )(
        tally, region, temp, temp.reshape(1, H), vmem(xin), vmem(w), vmem(fg), mine, theirs,
        e_in, pblk, part, cw, y, z,
    )


def points_kernel(first, number, tally_ref, gs_ref, w_ref, pq_ref, *refs):
    out_hbm, out_ref, sem = refs[-3:]
    steps = (block_count(tally_ref) + 1) >> 1

    def copy(k):
        at = pl.ds(pl.multiple_of((first + k) * STEP, STEP), STEP)
        return pltpu.make_async_copy(out_ref.at[k], out_hbm.at[at, :], sem.at[k])

    @pl.loop(0, number)
    def _(k):
        b = first + k

        @pl.when(b < steps)
        def _():
            grad = dot(pq_ref[:, 0:512], gs_ref[b], NN) + dot(pq_ref[:, 512:1024], w_ref[b], NN)
            out_ref[k] = grad.T.astype(bf16)

        @pl.when(b >= steps)
        def _():
            out_ref[k] = jnp.zeros((STEP, C), bf16)

        copy(k).start()

    @pl.loop(0, number)
    def _(k):
        copy(k).wait()


def points(tally, gs, w, pq, first, number, into=None):
    more = () if into is None else (into,)
    return pl.pallas_call(
        functools.partial(points_kernel, first, number),
        in_specs=[in_smem(), in_vmem(), in_vmem(), in_vmem()] + [in_hbm()] * len(more),
        out_specs=in_hbm(),
        out_shape=pltpu.HBM((BLOCKS * ROWS, C), bf16),
        scratch_shapes=[pltpu.VMEM((number, STEP, C), bf16), pltpu.SemaphoreType.DMA((number,))],
        input_output_aliases={4: 0} if more else {},
        compiler_params=SMALL,
        cost_estimate=pl.CostEstimate(
            flops=4 * number * STEP * HG * C, bytes_accessed=number * 2**20, transcendentals=0
        ),
        name="points",
    )(tally, vmem(gs), vmem(w), pq, *map(hbm, more))


def pieces_kernel(keep_ref, recv_ref, own_ref, p1_ref, p2_ref, p3_ref):
    z = lax.axis_index("pts") & 3

    def piece(k):
        at = pl.ds(pl.multiple_of(((z + k) & 3) * PIECE, 16), PIECE)
        return keep_ref[at, :] + recv_ref[at, :].astype(f32)

    own_ref[...] = piece(0)
    p1_ref[...] = piece(1).astype(bf16)
    p2_ref[...] = piece(2).astype(bf16)
    p3_ref[...] = piece(3).astype(bf16)


def pieces(keep, recv):
    spec = in_vmem()
    return pl.pallas_call(
        pieces_kernel,
        in_specs=[spec, spec],
        out_specs=[spec] * 4,
        out_shape=[jax.ShapeDtypeStruct((PIECE, C), f32)]
        + [jax.ShapeDtypeStruct((PIECE, C), bf16)] * 3,
        compiler_params=SMALL,
        name="pieces",
    )(keep, recv)


def final_kernel(mine_ref, theirs_ref, patch_ref, win_ref, slice_ref, temp_ref, wout_ref, buf_ref):
    core = lax.axis_index("grp")
    z = lax.axis_index("pts") & 3
    for ref, half in ((mine_ref, core), (theirs_ref, 1 - core)):
        for k in range(4):
            at = pl.multiple_of(half * HALF + ((z - k) & 3) * PIECE, 16)
            buf_ref[pl.ds(at, PIECE), :] = ref[k]
    win_ref[:, 0:256] = buf_ref[0:256, :].astype(f32)
    win_ref[:, 256:512] = buf_ref[256:512, :].astype(f32)
    wout_ref[...] = buf_ref[512:768, :].astype(f32)
    patch_ref[...] = buf_ref[768:1280, :].astype(f32)
    slice_ref[...] = buf_ref[1280:1312, 0:64].astype(f32)
    temp_ref[...] = buf_ref[1312:1328, 0:8].astype(f32)[0:1, :]


def final(mine, theirs):
    spec = in_vmem()
    return pl.pallas_call(
        final_kernel,
        in_specs=[spec, spec],
        out_specs=[spec] * 5,
        out_shape=[
            jax.ShapeDtypeStruct((PATCHES, C), f32),
            jax.ShapeDtypeStruct((C, 2 * C), f32),
            jax.ShapeDtypeStruct((D, G), f32),
            jax.ShapeDtypeStruct((1, H), f32),
            jax.ShapeDtypeStruct((C, C), f32),
        ],
        scratch_shapes=[pltpu.VMEM((BUF, C), bf16)],
        compiler_params=SMALL,
        name="final",
    )(mine, theirs)


def shift_pairs(dim, k):
    unit = (16, 4, 1)[dim]
    pairs = []
    for p in range(64):
        at = (p // unit) % 4
        pairs.append((p, p + ((at + k) % 4 - at) * unit))
    return pairs


def shift(v, dim, k):
    return lax.ppermute(v, "pts", shift_pairs(dim, k))


def swap(v):
    return lax.ppermute(v, "grp", [(0, 1), (1, 0)])


def ring_sum(v, dim):
    one, three, two = shift(v, dim, 1), shift(v, dim, 3), shift(v, dim, 2)
    return (v + two) + (one + three)


def ring_sum_b(v, dim):
    sent = v.astype(bf16)
    one, three, two = (shift(sent, dim, k).astype(f32) for k in (1, 3, 2))
    return lax.reduce_precision((v + two) + (one + three), 8, 7)


def shards(x, u, region, tally, lut, e_in, part, temp, triple, x_out):
    w, fg, xin, u_kept, keep, send, cw, pblk = first_sweep(
        x, u, region, tally, lut, e_in, x_out, part, temp
    )
    sums = keep + swap(send)
    sums = ring_sum(sums, 2)
    y = moment("xin_moment", tally, xin, w)
    sums, y = lax.optimization_barrier((sums, y))
    sums = ring_sum(sums, 1)
    z = moment("u_moment", tally, u_kept, w)
    sums, z = lax.optimization_barrier((sums, z))
    sums = ring_sum(sums, 0)
    mine = middle(sums, triple)
    theirs = swap(mine)
    w_qkv = (mine[192:224] + theirs[192:224])[:, 0:96]

    gs, pq, keep, send = second_sweep(
        tally, region, temp, xin, w, fg, mine, theirs, e_in, pblk, part, cw, y, z
    )
    own, p1, p2, p3 = pieces(keep, swap(send))
    r1, r2, r3 = shift(p1, 2, 1), shift(p2, 2, 2), shift(p3, 2, 3)
    grad_points = points(tally, gs, w, pq, 0, STEPS // 2)
    total = (own + r1.astype(f32)) + (r2.astype(f32) + r3.astype(f32))
    total = lax.reduce_precision(total, 8, 7)
    total, grad_points = lax.optimization_barrier((total, grad_points))
    total = ring_sum_b(total, 1)
    grad_points = points(tally, gs, w, pq, STEPS // 2, STEPS // 2, grad_points)
    total, grad_points = lax.optimization_barrier((total, grad_points))
    total = ring_sum_b(total, 0)
    mine = total.astype(bf16)
    mine = jnp.stack([mine] + [shift(mine, 2, k) for k in (1, 2, 3)])
    patch, w_in, w_slice, w_temp, w_out = final(mine, swap(mine))
    return grad_points, patch, w_in, w_slice, w_temp.reshape(H), w_qkv, w_out


def solution(mesh):
    rows = P(("pts", "grp"), None)
    return jax.shard_map(
        shards,
        mesh=mesh,
        in_specs=(rows, rows) + (P(),) * 8,
        out_specs=(rows,) + (P(),) * 6,
        check_vma=False,
    )
```

```python
import functools
import math

import jax
import jax.numpy as jnp
from jax import lax
from jax.experimental import pallas as pl
from jax.experimental.pallas import tpu as pltpu
from jax.sharding import PartitionSpec as P

f32 = jnp.float32
bf16 = jnp.bfloat16
HIGH = lax.Precision.HIGHEST
EPS = 1e-05
LOG2E = math.log2(math.e)

ROWS = 512
BLOCKS = 16
STEP = 1024
STEPS = BLOCKS * ROWS // STEP
UNROLL = 4
C = 256
H = 8
D = 32
G = 64
HG = H * G
PATCHES = 512
SUMS = 136
MID = 224
PIECE = 176
HALF = 4 * PIECE
BUF = 2 * HALF
EXT = C + BLOCKS
LANES = 256
CHUNKS = STEP // LANES
UNITS = (16, 4, 1)
AXES = ((2, 1, 0), (1, 0, 2))
VMEM_LIMIT = 16 * 2**20
SMALL = pltpu.CompilerParams(vmem_limit_bytes=8 * 2**20)

NN = (((1,), (0,)), ((), ()))
NT = (((1,), (1,)), ((), ()))
TN = (((0,), (0,)), ((), ()))


def dot(a, b, dims, precision=None):
    return lax.dot_general(a, b, dims, precision=precision, preferred_element_type=f32)


def split(a):
    hi = a.astype(bf16)
    return hi, (a - hi.astype(f32)).astype(bf16)


def split3(a):
    hi, rest = a.astype(bf16), a - a.astype(bf16).astype(f32)
    return (hi, *split(rest))


def dot_left2(a, b, dims):
    hi, lo = split(a)
    return dot(hi, b, dims) + dot(lo, b, dims)


def dot_right2(a, b, dims):
    hi, lo = split(b)
    return dot(a, hi, dims) + dot(a, lo, dims)


def dot3(a, b, dims):
    (a_hi, a_lo), (b_hi, b_lo) = split(a), split(b)
    return dot(a_hi, b_hi, dims) + (dot(a_hi, b_lo, dims) + dot(a_lo, b_hi, dims))


def iota(shape, dim):
    return lax.broadcasted_iota(jnp.int32, shape, dim)


def head_mask(j, rows):
    return (iota((rows, 128), 1) >> 5) == j


def spread(packed):
    return jnp.concatenate([jnp.where(head_mask(j, G), packed, 0.0) for j in range(4)], axis=0)


def gather_heads(wide):
    total = jnp.where(head_mask(0, G), wide[0:G], 0.0)
    for j in range(1, 4):
        total = total + jnp.where(head_mask(j, G), wide[j * G : (j + 1) * G], 0.0)
    return total


def in_vmem():
    return pl.BlockSpec(memory_space=pltpu.VMEM)


def in_smem():
    return pl.BlockSpec(memory_space=pltpu.SMEM)


def in_hbm():
    return pl.BlockSpec(memory_space=pl.ANY)


def hbm(v):
    return pltpu.with_memory_space_constraint(v, pltpu.HBM)


def vmem(v):
    return pltpu.with_memory_space_constraint(v, pltpu.VMEM)


def place():
    return lax.axis_index("pts"), lax.axis_index("grp")


def ring_place(core):
    pts = lax.axis_index("pts")
    return jnp.where(core == 0, pts // UNITS[AXES[0][0]], pts // UNITS[AXES[1][0]]) & 3


def block_count(tally_ref):
    pts, grp = place()
    return tally_ref[grp, pts]


def step_count(tally_ref):
    return ((block_count(tally_ref) + 2 * UNROLL - 1) // (2 * UNROLL)) * UNROLL


def patch_onehot(region_ref):
    pts, grp = place()
    mine = iota((BLOCKS, 64), 1) == pts
    ids = jnp.sum(jnp.where(mine, region_ref[grp], 0), axis=1, keepdims=True)
    return (iota((BLOCKS, PATCHES), 1) == ids).astype(f32)


def first_kernel(
    tally_hbm,
    region_hbm,
    x_hbm,
    u_hbm,
    lut_hbm,
    e_in_hbm,
    x_out_hbm,
    p_hbm,
    temp_hbm,
    w_ref,
    fg_ref,
    xt_ref,
    u_ref,
    keep_ref,
    send_ref,
    pblk_ref,
    tally_ref,
    region_ref,
    temp_ref,
    x_ref,
    lut_ref,
    e_in_ref,
    x_out_ref,
    p_ref,
    et_ref,
    rows_ref,
    acc_ref,
    x_sem,
    u_sem,
    sem,
):
    small = [
        pltpu.make_async_copy(src, dst, sem.at[k])
        for k, (src, dst) in enumerate(
            (
                (e_in_hbm, e_in_ref),
                (p_hbm, p_ref),
                (lut_hbm, lut_ref),
                (x_out_hbm, x_out_ref),
                (temp_hbm, temp_ref),
                (tally_hbm, tally_ref),
                (region_hbm, region_ref),
            )
        )
    ]
    for copy in small:
        copy.start()

    def rows_copies(b):
        at = pl.ds(b * STEP if isinstance(b, int) else pl.multiple_of(b * STEP, STEP), STEP)
        return (
            pltpu.make_async_copy(x_hbm.at[at, :], x_ref.at[b], x_sem.at[b]),
            pltpu.make_async_copy(u_hbm.at[at, :], u_ref.at[b], u_sem.at[b]),
        )

    for b in range(STEPS):
        for copy in rows_copies(b):
            copy.start()

    acc_ref[...] = jnp.zeros_like(acc_ref)
    for b in range(STEPS):
        block = 2 * b + (iota((BLOCKS, STEP), 1) >> 9)
        xt_ref[b, C:EXT, :] = (iota((BLOCKS, STEP), 0) == block).astype(f32).astype(bf16)
        for q in range(2):
            fg_ref[b, q, C:EXT, :] = jnp.ones((BLOCKS, STEP), bf16)
    for copy in small:
        copy.wait()
    count = block_count(tally_ref)
    steps = step_count(tally_ref)
    onehot = patch_onehot(region_ref).astype(bf16)
    et_ref[...] = e_in_ref[...].T
    t1 = ((iota((HG, G), 0) & (G - 1)) == iota((HG, G), 1)).astype(f32).astype(bf16)
    t2 = (iota((D, C), 0) == (iota((D, C), 1) & (D - 1))).astype(f32).astype(bf16)
    tall = dot(t1, p_ref[...], NT).astype(bf16)
    tiled = dot(tall, t2, NN)
    own = (iota((HG, C), 0) >> 6) == (iota((HG, C), 1) >> 5)
    pblk_ref[...] = jnp.where(own, tiled, 0.0).astype(bf16)
    rows_ref[...] = dot(onehot, lut_ref[...], NN)

    def project(b, c):
        at = pl.ds(c * LANES, LANES)
        block = 2 * b + c * LANES // ROWS
        xin = x_ref[b, at, :] + rows_ref[pl.ds(block, 1), :].astype(bf16)
        xt_ref[b, 0:C, at] = xin.T
        proj = dot(et_ref[...], xin, NT).astype(bf16)
        grad_y = dot(x_out_ref[...], u_ref[b, at, :], NT).astype(bf16)
        for q in range(2):
            fg_ref[b, q, 0:128, at] = proj[256 + 128 * q : 384 + 128 * q]
            fg_ref[b, q, 128:256, at] = grad_y[128 * q : 128 * q + 128]
        return dot(pblk_ref[...], proj[0:C], NN)

    def soften(b, c, logits):
        lo = c * LANES
        valid = (iota((1, LANES), 1) + (b * STEP + lo) < count * ROWS).astype(f32)
        for h in range(H):
            at = pl.ds(h * G, G)
            scale = LOG2E / jnp.full((1, LANES), temp_ref[h], f32)
            part = logits[G * h : G * h + G]
            top = jnp.max(part, axis=0, keepdims=True)
            ex = jnp.exp2((part - top) * scale)
            wt = ex * (valid / jnp.sum(ex, axis=0, keepdims=True))
            w_ref[b, at, lo : lo + LANES] = wt.astype(bf16)

    @pl.loop(0, steps, step=UNROLL)
    def _(i):
        order = [(i + k, c) for k in range(UNROLL) for c in range(CHUNKS)]
        for k in range(UNROLL):
            for copy in rows_copies(i + k):
                copy.wait()
        logits = project(*order[0])
        for k, (b, c) in enumerate(order):
            following = project(*order[k + 1]) if k + 1 < len(order) else None
            soften(b, c, logits)
            logits = following
            if c == CHUNKS - 1:
                for q in range(2):
                    at = pl.ds(256 * q, 256)
                    acc_ref[q] += dot(fg_ref[b, q], w_ref[b, at, :], NT)

    @pl.loop(steps, STEPS)
    def _(b):
        for copy in rows_copies(b):
            copy.wait()

    core = lax.axis_index("grp")
    for q in range(2):
        raw = gather_heads(acc_ref[q, 0:128, :].T)
        grad = gather_heads(acc_ref[q, 128:256, :].T)
        norm = acc_ref[q, C : C + 8, :]
        row = iota((8, 128), 0)
        norm = jnp.where(row == 0, norm[:, 0:128], jnp.where(row == 1, norm[:, 128:256], 0.0))

        def put(ref):
            ref[0:64, :] = raw
            ref[64:128, :] = grad
            ref[128:136, :] = norm

        pl.when(core == q)(lambda: put(keep_ref))
        pl.when(core != q)(lambda: put(send_ref))


def first_sweep(x, u, region, tally, lut, e_in, x_out, part, temp):
    return pl.pallas_call(
        first_kernel,
        in_specs=[in_hbm()] * 9,
        out_specs=[in_vmem()] * 7,
        scratch_shapes=[
            pltpu.SMEM((2, 64), jnp.int32),
            pltpu.VMEM((2, BLOCKS, 64), jnp.int32),
            pltpu.SMEM((H,), f32),
            pltpu.VMEM((STEPS, STEP, C), bf16),
            pltpu.VMEM((PATCHES, C), bf16),
            pltpu.VMEM((C, 2 * C), bf16),
            pltpu.VMEM((C, C), bf16),
            pltpu.VMEM((D, G), bf16),
            pltpu.VMEM((2 * C, C), bf16),
            pltpu.VMEM((BLOCKS, C), f32),
            pltpu.VMEM((2, EXT, 256), f32),
            pltpu.SemaphoreType.DMA((STEPS,)),
            pltpu.SemaphoreType.DMA((STEPS,)),
            pltpu.SemaphoreType.DMA((7,)),
        ],
        out_shape=[
            pltpu.VMEM((STEPS, HG, STEP), bf16),
            pltpu.VMEM((STEPS, 2, EXT, STEP), bf16),
            pltpu.VMEM((STEPS, EXT, STEP), bf16),
            pltpu.VMEM((STEPS, STEP, C), bf16),
            jax.ShapeDtypeStruct((SUMS, 128), f32),
            jax.ShapeDtypeStruct((SUMS, 128), f32),
            jax.ShapeDtypeStruct((HG, C), bf16),
        ],
        compiler_params=pltpu.CompilerParams(vmem_limit_bytes=VMEM_LIMIT),
        name="first_sweep",
    )(*map(hbm, (tally, region, x, u, lut, e_in, x_out, part, temp)))


def xin_moment_kernel(lo, hi, tally_ref, xt_ref, w_ref, out_ref):
    out_ref[...] = jnp.zeros_like(out_ref)

    @pl.loop(lo, jnp.minimum(hi, step_count(tally_ref)))
    def _(b):
        out_ref[...] += dot(xt_ref[b], w_ref[b], NT)


def u_moment_kernel(lo, hi, tally_ref, u_ref, w_ref, out_ref):
    out_ref[...] = jnp.zeros_like(out_ref)

    @pl.loop(lo, jnp.minimum(hi, step_count(tally_ref)))
    def _(b):
        out_ref[...] += dot(w_ref[b], u_ref[b], NN)


def moment(kernel, shape, lo, hi, tally, rows, w):
    return pl.pallas_call(
        functools.partial(kernel, lo, hi),
        in_specs=[in_smem(), in_vmem(), in_vmem()],
        out_specs=in_vmem(),
        out_shape=pltpu.VMEM(shape, f32),
        compiler_params=SMALL,
        cost_estimate=pl.CostEstimate(
            flops=2 * (hi - lo) * STEP * HG * C, bytes_accessed=(hi - lo) * 2**20, transcendentals=0
        ),
        name="moment",
    )(tally, vmem(rows), vmem(w))


def middle_kernel(s_ref, t_ref, out_ref):
    raw = s_ref[0:64, :]
    grad = s_ref[64:128, :]
    norm = jnp.concatenate([s_ref[128:136, :], jnp.zeros((120, 128), f32)], axis=0).T
    denom = jnp.full((G, 128), EPS, f32)
    for j in range(4):
        col = norm[G * (j % 2) : G * (j % 2) + G, j // 2 : j // 2 + 1]
        denom = denom + jnp.where(head_mask(j, G), col, 0.0)
    inv = 1.0 / denom
    token = raw * inv
    t2 = (iota((D, 128), 0) == (iota((D, 128), 1) & (D - 1))).astype(f32).astype(bf16)
    own = (iota((128, 128), 0) >> 5) == (iota((128, 128), 1) >> 5)
    triple = t_ref[...]

    def diagonal(k):
        wide = dot(triple[:, D * k : D * k + D], t2, NN)
        return jnp.where(own, jnp.concatenate([wide] * 4, axis=0), 0.0).astype(bf16)

    wq, wk, wv = diagonal(0), diagonal(1), diagonal(2)
    query = dot_left2(token, wq, NN)
    keys = dot_left2(token, wk, NN)
    values = dot_left2(token, wv, NN)
    rate = 1.0 / math.sqrt(D)
    query_s = spread(query)
    scores = dot3(query_s, keys, NT) * rate
    scores = jnp.exp(scores - jnp.max(scores, axis=1, keepdims=True))
    probs = scores / jnp.sum(scores, axis=1, keepdims=True)
    out = gather_heads(dot3(probs, values, NN))
    grad_s = spread(grad)
    d_values = dot3(probs.T, grad_s, NN)
    d_probs = dot3(grad_s, values, NT)
    d_scores = probs * (d_probs - jnp.sum(d_probs * probs, axis=1, keepdims=True)) * rate
    d_query = gather_heads(dot3(d_scores, keys, NN))
    d_keys = dot3(d_scores.T, query_s, NN)
    d_token = (
        dot_left2(d_query, wq, NT) + dot_left2(d_keys, wk, NT) + dot_left2(d_values, wv, NT)
    )
    grad_raw = d_token * inv
    group = ((iota((128, 128), 0) >> 5) == iota((128, 128), 1)).astype(f32)
    first = (iota((128, 128), 1) < 4).astype(f32)
    grad_norm = -dot_left2(d_token * token * inv, (group * first).astype(bf16), NN)
    out_ref[0:64, :] = out.astype(bf16).astype(f32)
    out_ref[64:128, :] = grad_raw.astype(bf16).astype(f32)
    out_ref[128:192, :] = grad_norm
    token_t = jnp.concatenate([token, jnp.zeros((64, 128), f32)], axis=0).T[:, 0:64]
    total = jnp.zeros((D, 128), f32)
    for k, d_part in enumerate((d_query, d_keys, d_values)):
        full = jnp.where(own, dot3(token_t, d_part, NN), 0.0)
        full = full[0:32] + full[32:64] + (full[64:96] + full[96:128])
        fold = ((iota((128, 128), 0) & (D - 1)) + D * k == iota((128, 128), 1)).astype(f32)
        total = total + dot_left2(full, fold.astype(bf16), NN)
    out_ref[192:224, :] = total


def middle(sums, triple):
    return pl.pallas_call(
        middle_kernel,
        out_shape=jax.ShapeDtypeStruct((MID, 128), f32),
        compiler_params=SMALL,
        name="middle",
    )(sums, triple)


def second_kernel(
    tally_ref,
    region_ref,
    temp_ref,
    temp_row_ref,
    xt_ref,
    w_ref,
    fg_ref,
    mine_ref,
    theirs_ref,
    e_in_ref,
    pblk_ref,
    p_ref,
    y1_ref,
    y2_ref,
    z1_ref,
    z2_ref,
    gs_ref,
    pq_ref,
    keep_ref,
    send_ref,
    og_ref,
    gn_ref,
    v_ref,
    ob_ref,
    gr_ref,
    buf_ref,
):
    steps = step_count(tally_ref)
    core = lax.axis_index("grp")

    def prologue():
        for q in range(2):
            at = pl.ds(256 * q, 256)
            mine = core == q
            out_b = jnp.where(mine, mine_ref[0:64, :], theirs_ref[0:64, :])
            grad_raw = jnp.where(mine, mine_ref[64:128, :], theirs_ref[64:128, :])
            grad_norm = jnp.where(mine, mine_ref[128:192, :], theirs_ref[128:192, :])
            grad_norm = grad_norm - jnp.mean(grad_norm, axis=0, keepdims=True)
            for j in range(4):
                gn_ref[pl.ds(256 * q + G * j, G), :] = jnp.broadcast_to(
                    grad_norm[:, j : j + 1], (G, 128)
                ) / jnp.full((1, 128), temp_ref[4 * q + j], f32)
            cols = pl.ds(128 * q, 128)
            off = slice(0, 256) if q else slice(256, 512)
            zero = jnp.zeros((256, 128), bf16)
            ob_ref[at, cols] = spread(out_b).astype(bf16)
            gr_ref[at, cols] = spread(grad_raw).astype(bf16)
            ob_ref[off, cols] = zero
            gr_ref[off, cols] = zero
            sharp = jnp.full((1, 128), temp_ref[4 * q], f32)
            for j in range(1, 4):
                sharp = jnp.where(head_mask(j, 1), temp_ref[4 * q + j], sharp)
            og_ref[at, 0:128] = spread(
                (grad_raw - jnp.mean(grad_raw, axis=0, keepdims=True)) / sharp
            ).astype(bf16)
            og_ref[at, 128:256] = spread(
                (out_b - jnp.mean(out_b, axis=0, keepdims=True)) / sharp
            ).astype(bf16)
        v_ref[...] = jnp.zeros_like(v_ref)

    prologue()

    def grad_weights(b, c):
        at = [pl.ds(256 * q, 256) for q in range(2)]
        lanes = pl.ds(c * LANES, LANES)
        return [dot(og_ref[at[q], :], fg_ref[b, q, 0:C, lanes], NN) for q in range(2)]

    def grad_slices(b, c, grad_w):
        lanes = pl.ds(c * LANES, LANES)
        for h in range(H):
            at = pl.ds(h * G, G)
            col = jnp.concatenate([gn_ref[at, :]] * (LANES // 128), axis=1)
            j = G * (h & 3)
            wt = w_ref[b, at, lanes].astype(f32)
            wg = wt * (grad_w[h >> 2][j : j + G] + col)
            gs = wg - wt * jnp.sum(wg, axis=0, keepdims=True)
            gs_ref[b, at, lanes] = gs.astype(bf16)

    @pl.loop(0, steps, step=UNROLL)
    def _(i):
        order = [(i + k, c) for k in range(UNROLL) for c in range(CHUNKS)]
        grad_w = grad_weights(*order[0])
        for k, (b, c) in enumerate(order):
            following = grad_weights(*order[k + 1]) if k + 1 < len(order) else None
            grad_slices(b, c, grad_w)
            grad_w = following
            if c == CHUNKS - 1:
                v_ref[...] += dot(xt_ref[b], gs_ref[b], NT)

    v = v_ref[...]
    y = y1_ref[...] + y2_ref[...]
    pblk = pblk_ref[...]
    gr = gr_ref[...]
    pq_ref[:, 0:512] = dot(e_in_ref[:, 0:256], pblk, NT).astype(bf16)
    pq_ref[:, 512:1024] = dot(e_in_ref[:, 256:512], gr, NT).astype(bf16)
    buf_ref[0:256, :] = dot_left2(v[0:C], pblk, NN)
    buf_ref[256:512, :] = dot_left2(y[0:C], gr, NN)
    buf_ref[512:768, :] = dot_right2(ob_ref[...].astype(f32).T.astype(bf16), z1_ref[...] + z2_ref[...], NN)
    onehot = patch_onehot(region_ref).T.astype(bf16)
    per_block = dot_left2(v[C:EXT], pq_ref[:, 0:512], NT)
    per_block = per_block + dot_left2(y[C:EXT], pq_ref[:, 512:1024], NT)
    buf_ref[768:1280, :] = dot_right2(onehot, per_block, NN)
    et = e_in_ref[:, 0:256].T
    cross = dot_right2(et, v[0:C], NN)
    own = (iota((256, 512), 0) >> 5) == (iota((256, 512), 1) >> 6)
    cross = jnp.where(own, cross, 0.0)
    heads = cross[0:32]
    for k in range(1, 8):
        heads = heads + cross[32 * k : 32 * k + 32]
    by_slice = (heads[:, 0:128] + heads[:, 128:256]) + (heads[:, 256:384] + heads[:, 384:512])
    by_slice = by_slice + pltpu.roll(by_slice, G, 1)
    tile = (iota((G, HG), 0) == (iota((G, HG), 1) & (G - 1))).astype(f32).astype(bf16)
    by_head = ((iota((HG, 8), 0) >> 6) == iota((HG, 8), 1)).astype(f32).astype(bf16)
    weighed = heads * dot(p_ref[...], tile, NN)
    weighed = jnp.broadcast_to(jnp.sum(weighed, axis=0, keepdims=True), (8, HG))
    hi, mid, lo = split3(weighed)
    sharp = dot(hi, by_head, NN) + (dot(mid, by_head, NN) + dot(lo, by_head, NN))
    sharp = -sharp / temp_row_ref[...]
    buf_ref[1280:BUF, :] = jnp.zeros((BUF - 1280, 256), f32)
    buf_ref[1280:1312, 0:128] = by_slice
    buf_ref[1312:1320, 0:8] = sharp
    keep_ref[...] = buf_ref[pl.ds(pl.multiple_of(core * HALF, 16), HALF), :]
    send_ref[...] = buf_ref[
        pl.ds(pl.multiple_of((1 - core) * HALF, 16), HALF), :
    ].astype(bf16)


def second_sweep(tally, region, temp, xt, w, fg, mine, theirs, e_in, pblk, part, *moments):
    return pl.pallas_call(
        second_kernel,
        in_specs=[in_smem(), in_vmem(), in_smem()] + [in_vmem()] * 13,
        out_specs=[in_vmem()] * 4,
        scratch_shapes=[
            pltpu.VMEM((HG, 256), bf16),
            pltpu.VMEM((HG, 128), f32),
            pltpu.VMEM((EXT, HG), f32),
            pltpu.VMEM((HG, C), bf16),
            pltpu.VMEM((HG, C), bf16),
            pltpu.VMEM((BUF, C), f32),
        ],
        out_shape=[
            pltpu.VMEM((STEPS, HG, STEP), bf16),
            pltpu.VMEM((C, 1024), bf16),
            pltpu.VMEM((HALF, C), f32),
            pltpu.VMEM((HALF, C), bf16),
        ],
        compiler_params=pltpu.CompilerParams(vmem_limit_bytes=VMEM_LIMIT),
        name="second_sweep",
    )(
        tally, region, temp, temp.reshape(1, H), vmem(xt), vmem(w), vmem(fg), mine, theirs,
        e_in, pblk, part, *map(vmem, moments),
    )


def points_kernel(first, number, tally_ref, gs_ref, w_ref, pq_ref, *refs):
    out_hbm, out_ref, sem = refs[-3:]
    steps = step_count(tally_ref)

    def copy(k):
        at = pl.ds(pl.multiple_of((first + k) * STEP, STEP), STEP)
        return pltpu.make_async_copy(out_ref.at[k], out_hbm.at[at, :], sem.at[k])

    @pl.loop(0, number)
    def _(k):
        b = first + k

        @pl.when(b < steps)
        def _():
            grad = dot(pq_ref[:, 0:512], gs_ref[b], NN) + dot(pq_ref[:, 512:1024], w_ref[b], NN)
            out_ref[k] = grad.T.astype(bf16)

        @pl.when(b >= steps)
        def _():
            out_ref[k] = jnp.zeros((STEP, C), bf16)

        copy(k).start()

    @pl.loop(0, number)
    def _(k):
        copy(k).wait()


def points(tally, gs, w, pq, first, number, into=None):
    more = () if into is None else (into,)
    return pl.pallas_call(
        functools.partial(points_kernel, first, number),
        in_specs=[in_smem(), in_vmem(), in_vmem(), in_vmem()] + [in_hbm()] * len(more),
        out_specs=in_hbm(),
        out_shape=pltpu.HBM((BLOCKS * ROWS, C), bf16),
        scratch_shapes=[pltpu.VMEM((number, STEP, C), bf16), pltpu.SemaphoreType.DMA((number,))],
        input_output_aliases={4: 0} if more else {},
        compiler_params=SMALL,
        cost_estimate=pl.CostEstimate(
            flops=4 * number * STEP * HG * C, bytes_accessed=number * 2**20, transcendentals=0
        ),
        name="points",
    )(tally, vmem(gs), vmem(w), vmem(pq), *map(hbm, more))


def pieces_kernel(keep_ref, recv_ref, own_ref, p1_ref, p2_ref, p3_ref):
    z = ring_place(lax.axis_index("grp"))

    def piece(k):
        at = pl.ds(pl.multiple_of((z ^ k) * PIECE, 16), PIECE)
        return keep_ref[at, :] + recv_ref[at, :].astype(f32)

    own_ref[...] = piece(0)
    p1_ref[...] = piece(1).astype(bf16)
    p2_ref[...] = piece(2).astype(bf16)
    p3_ref[...] = piece(3).astype(bf16)


def pieces(keep, recv):
    spec = in_vmem()
    return pl.pallas_call(
        pieces_kernel,
        in_specs=[spec, spec],
        out_specs=[spec] * 4,
        out_shape=[jax.ShapeDtypeStruct((PIECE, C), f32)]
        + [jax.ShapeDtypeStruct((PIECE, C), bf16)] * 3,
        compiler_params=SMALL,
        name="pieces",
    )(vmem(keep), recv)


def final_kernel(mine_ref, theirs_ref, patch_ref, win_ref, slice_ref, temp_ref, wout_ref, buf_ref):
    core = lax.axis_index("grp")
    for ref, half in ((mine_ref, core), (theirs_ref, 1 - core)):
        z = ring_place(half)
        for k in range(4):
            at = pl.multiple_of(half * HALF + (z ^ k) * PIECE, 16)
            buf_ref[pl.ds(at, PIECE), :] = ref[k]
    win_ref[:, 0:256] = buf_ref[0:256, :].astype(f32)
    win_ref[:, 256:512] = buf_ref[256:512, :].astype(f32)
    wout_ref[...] = buf_ref[512:768, :].astype(f32)
    patch_ref[...] = buf_ref[768:1280, :].astype(f32)
    slice_ref[...] = buf_ref[1280:1312, 0:64].astype(f32)
    temp_ref[...] = buf_ref[1312:1328, 0:8].astype(f32)[0:1, :]


def final(mine, theirs):
    spec = in_vmem()
    return pl.pallas_call(
        final_kernel,
        in_specs=[spec, spec],
        out_specs=[spec] * 5,
        out_shape=[
            jax.ShapeDtypeStruct((PATCHES, C), f32),
            jax.ShapeDtypeStruct((C, 2 * C), f32),
            jax.ShapeDtypeStruct((D, G), f32),
            jax.ShapeDtypeStruct((1, H), f32),
            jax.ShapeDtypeStruct((C, C), f32),
        ],
        scratch_shapes=[pltpu.VMEM((BUF, C), bf16)],
        compiler_params=SMALL,
        name="final",
    )(mine, theirs)


def shift_pairs(step, k):
    pairs = []
    for device in range(128):
        unit = UNITS[AXES[device % 2][step]] * 2
        at = (device // unit) % 4
        pairs.append((device, device + ((at ^ k) - at) * unit))
    return pairs


def shift(v, step, k):
    return lax.ppermute(v, ("pts", "grp"), shift_pairs(step, k))


def swap(v):
    return lax.ppermute(v, "grp", [(0, 1), (1, 0)])


def ring_sum(v, step):
    one, three, two = shift(v, step, 1), shift(v, step, 3), shift(v, step, 2)
    return (v + two) + (one + three)


def ring_sum_b(v, step):
    sent = v.astype(bf16)
    one, three, two = (shift(sent, step, k).astype(f32) for k in (1, 3, 2))
    return lax.reduce_precision((v + two) + (one + three), 8, 7)


def shards(x, u, region, tally, lut, e_in, part, temp, triple, x_out):
    tally, region = tally.T, region.transpose(1, 2, 0)
    w, fg, xt, u_kept, keep, send, pblk = first_sweep(
        x, u, region, tally, lut, e_in, x_out, part, temp
    )
    sums = keep + swap(send)
    third = STEPS // 4
    sums = ring_sum(sums, 0)
    y1 = moment(xin_moment_kernel, (EXT, HG), 0, STEPS - third, tally, xt, w)
    sums, y1 = lax.optimization_barrier((sums, y1))
    sums = ring_sum(sums, 1)
    y2 = moment(xin_moment_kernel, (EXT, HG), STEPS - third, STEPS, tally, xt, w)
    z1 = moment(u_moment_kernel, (HG, C), 0, third, tally, u_kept, w)
    sums, y2, z1 = lax.optimization_barrier((sums, y2, z1))
    sums = ring_sum(sums, 2)
    z2 = moment(u_moment_kernel, (HG, C), third, STEPS, tally, u_kept, w)
    sums, z2 = lax.optimization_barrier((sums, z2))
    mine = middle(sums, triple)
    theirs = swap(mine)
    w_qkv = (mine[192:224] + theirs[192:224])[:, 0:96]

    gs, pq, keep, send = second_sweep(
        tally, region, temp, xt, w, fg, mine, theirs, e_in, pblk, part, y1, y2, z1, z2
    )
    own, p1, p2, p3 = pieces(keep, swap(send))
    part_steps = STEPS // 4

    def rows_beside(total, done, k):
        done = points(tally, gs, w, pq, k * part_steps, part_steps, done)
        return lax.optimization_barrier((total, done))

    r1, r2, r3 = shift(p1, 0, 1), shift(p2, 0, 2), shift(p3, 0, 3)
    total = (own + r1.astype(f32)) + (r2.astype(f32) + r3.astype(f32))
    total = lax.reduce_precision(total, 8, 7)
    total, grad_points = rows_beside(total, None, 0)
    total = ring_sum_b(total, 1)
    total, grad_points = rows_beside(total, grad_points, 1)
    total = ring_sum_b(total, 2)
    total, grad_points = rows_beside(total, grad_points, 2)
    mine = total.astype(bf16)
    mine = jnp.stack([mine] + [shift(mine, 0, k) for k in (1, 2, 3)])
    mine, grad_points = rows_beside(mine, grad_points, 3)
    patch, w_in, w_slice, w_temp, w_out = final(mine, swap(mine))
    return grad_points, patch, w_in, w_slice, w_temp.reshape(H), w_qkv, w_out


def solution(mesh):
    rows = P(("pts", "grp"), None)
    return jax.shard_map(
        shards,
        mesh=mesh,
        in_specs=(rows, rows) + (P(),) * 8,
        out_specs=(rows,) + (P(),) * 6,
        check_vma=False,
    )
```
